32 devices in a mesh: group: 4 (over x, core), dev: 8 (over z, y).
Axes of the slice: x: 2, y: 2, z: 4, core: 2. Of those that a mesh axis runs over, the one named last changes fastest.
Arguments:
- state: float32 [5, 4, 4, 4, 8, 16, 128], P(None, None, None, None, 'group', 'dev'), may hold values from -3 to 19.25, as said below
- limit_slot: int32 [8, 16, 128], P('group', 'dev'), may hold values from -1 to 127, as said below
- wall_owner: int32 [8, 16, 2], P('group', 'dev'), may hold values from 0 to 255
Outputs:
- state_next: float32 [5, 4, 4, 4, 8, 16, 128], P(None, None, None, None, 'group', 'dev')
- wall_loads: float32 [256], P(('group', 'dev'))
The draws below stay inside these ranges and needn't reach their ends.
Inputs may be any that keep to these rules, and one draw needn't show every extreme that they name: `state`: density lies in 0.5 to 2, each velocity component in -1.5 to 1.5 and p in 0.2 to 5 at every node. A troubled element has limit_slot = destination * 16 + slot, the destination an index of dev within the element's group and the slot below 16. The troubled elements of one device have distinct values and fill whole blocks of 16 slots per destination; one device has at most 128 troubled elements, some device of every group has exactly 128, and every device is the destination of exactly 32 troubled elements of its group.
All inputs are finite; a program needn't handle non-finite values.
Results may differ from the reference program's by a relative error of at most 0.00013.
Values sent between devices are 32-bit elements; how exact they have to be, the bound alone decides.
A program may use at most 64 MiB of HBM per device.

```python
import jax
import jax.numpy as jnp
import numpy as np
from jax import lax

SUBSTEPS = 8
EX = 2
EY = 2
NZ = 128
CAP = 16
NX = 8
NY = 16
SNODES = 256


def draw_state(key, part):
    keys = jax.random.split(key, 3)
    field_shape = (4, 4, 4, NX, NY, NZ)
    density = jnp.exp(jax.random.uniform(keys[0], field_shape, jnp.float32, jnp.log(0.5), jnp.log(2.0)))
    velocity = jnp.clip(0.5 * jax.random.normal(keys[1], (3,) + field_shape, jnp.float32), -1.5, 1.5)
    pressure = jnp.exp(jax.random.uniform(keys[2], field_shape, jnp.float32, jnp.log(0.2), jnp.log(5.0)))
    kinetic = 0.5 * density * (velocity[0] * velocity[0] + velocity[1] * velocity[1] + velocity[2] * velocity[2])
    energy = pressure / 0.4 + kinetic
    return jnp.stack([density, density * velocity[0], density * velocity[1], density * velocity[2], energy]).astype(jnp.float32)


def draw_limit_slot(key, part):
    n_group = NX // EX
    n_dev = NY // EY
    per_device = EX * EY * NZ
    blocks_of = jnp.where(jnp.arange(n_dev, dtype=jnp.int32) < n_dev // 4, n_dev, 0).astype(jnp.int32)

    def one_group(group_key):
        order_key, offset_key, rank_key = jax.random.split(group_key, 3)
        source_order = jax.random.permutation(order_key, n_dev)
        starts = jax.random.randint(offset_key, (n_dev,), 0, n_dev)
        position = jnp.zeros(n_dev, jnp.int32).at[source_order].set(jnp.arange(n_dev, dtype=jnp.int32))
        source_blocks = blocks_of[position]
        source_start = starts[position]
        element_rank = jax.vmap(lambda device_key: jax.random.permutation(device_key, per_device))(jax.random.split(rank_key, n_dev))
        troubled = element_rank < source_blocks[:, None] * CAP
        destination = (source_start[:, None] + element_rank // CAP) % n_dev
        return jnp.where(troubled, destination * CAP + element_rank % CAP, -1)
    values = jax.vmap(one_group)(jax.random.split(key, n_group))
    values = values.reshape(n_group, n_dev, EX, EY, NZ).transpose(0, 2, 1, 3, 4).reshape(NX, NY, NZ)
    return values.astype(jnp.int32)


def set_ends(result, stream_key, low, top_value):
    longest = result.shape.index(max(result.shape))
    spots = []
    for shift in (0, 1):
        where = [jax.random.randint(jax.random.fold_in(stream_key, axis), (), 0, length) for axis, length in enumerate(result.shape)]
        where[longest] = (where[longest] + shift) % result.shape[longest]
        spots.append(tuple(where))
    return result.at[spots[0]].set(low).at[spots[1]].set(top_value)


def setup_inputs(seed: int = 0) -> dict:
    arg_keys = jax.random.split(jax.random.key(seed), 4)
    state = draw_state(jax.random.fold_in(arg_keys[3], 71), 0)
    limit_slot = draw_limit_slot(jax.random.fold_in(arg_keys[3], 71), 0)
    wall_owner = set_ends(jax.random.randint(arg_keys[2], (NX, NY, 2), 0, SNODES), jax.random.fold_in(arg_keys[2], 1), 0, SNODES - 1).astype(jnp.int32)
    return dict(state=state, limit_slot=limit_slot, wall_owner=wall_owner)


gamma_ratio = 1.4
courant = 0.02

def gll_tables():
    gll_nodes = np.array([-1.0, -np.sqrt(0.2), np.sqrt(0.2), 1.0])
    weights = np.array([1.0, 5.0, 5.0, 1.0]) / 6.0
    bary_weights = np.array([1.0 / np.prod([gll_nodes[index_a] - gll_nodes[index_b] for index_b in range(4) if index_b != index_a]) for index_a in range(4)])
    derivative = np.zeros((4, 4))
    for index_a in range(4):
        for index_b in range(4):
            if index_a != index_b:
                derivative[index_a, index_b] = bary_weights[index_b] / bary_weights[index_a] / (gll_nodes[index_a] - gll_nodes[index_b])
        derivative[index_a, index_a] = -np.sum(derivative[index_a])
    return (jnp.asarray(derivative, jnp.float32), jnp.asarray(weights, jnp.float32))

def euler_flux(conserved, direction):
    density = conserved[0]
    normal_velocity = conserved[1 + direction] / density
    pressure = (gamma_ratio - 1.0) * (conserved[4] - 0.5 * (conserved[1] * conserved[1] + conserved[2] * conserved[2] + conserved[3] * conserved[3]) / density)
    flux_rows = [conserved[1 + direction]]
    for component in range(3):
        momentum_flux = conserved[1 + component] * normal_velocity
        if component == direction:
            momentum_flux = momentum_flux + pressure
        flux_rows.append(momentum_flux)
    flux_rows.append(normal_velocity * (conserved[4] + pressure))
    wave_speed = jnp.abs(normal_velocity) + jnp.sqrt(gamma_ratio * pressure / density)
    return (jnp.stack(flux_rows), wave_speed)

def rusanov(left_state, right_state, direction):
    left_flux, left_speed = euler_flux(left_state, direction)
    right_flux, right_speed = euler_flux(right_state, direction)
    fastest = jnp.maximum(left_speed, right_speed)
    return 0.5 * (left_flux + right_flux) - 0.5 * fastest * (right_state - left_state)

def mirrored(conserved):
    return jnp.concatenate([conserved[:3], -conserved[3:4], conserved[4:]], axis=0)

def node_index(node_axis, which):
    return (slice(None),) * node_axis + (which,)

def dg_rate(state, direction, flux_low, flux_high, derivative, weights):
    node_flux, wave_speed = euler_flux(state, direction)
    einsum_forms = ['ai,vijk...->vajk...', 'aj,vijk...->viak...', 'ak,vijk...->vija...']
    volume = jnp.einsum(einsum_forms[direction], derivative, node_flux, precision=lax.Precision.HIGHEST)
    node_axis = 1 + direction
    low_index = node_index(node_axis, 0)
    high_index = node_index(node_axis, 3)
    volume = volume.at[low_index].add(-(flux_low - node_flux[low_index]) / weights[0])
    volume = volume.at[high_index].add((flux_high - node_flux[high_index]) / weights[3])
    return volume

def fv_rate(state, direction, flux_low, flux_high, weights):
    node_axis = 1 + direction
    lower_nodes = lax.slice_in_dim(state, 0, 3, axis=node_axis)
    upper_nodes = lax.slice_in_dim(state, 1, 4, axis=node_axis)
    inner_flux = rusanov(lower_nodes, upper_nodes, direction)
    interfaces = jnp.concatenate([jnp.expand_dims(flux_low, node_axis), inner_flux, jnp.expand_dims(flux_high, node_axis)], axis=node_axis)
    width_shape = [1] * state.ndim
    width_shape[node_axis] = 4
    widths = weights.reshape(width_shape)
    upper_faces = lax.slice_in_dim(interfaces, 1, 5, axis=node_axis)
    lower_faces = lax.slice_in_dim(interfaces, 0, 4, axis=node_axis)
    return (upper_faces - lower_faces) / widths

def dg_next(state, fluxes, derivative, weights):
    rate_sum = dg_rate(state, 0, fluxes[0], fluxes[1], derivative, weights)
    rate_sum = rate_sum + dg_rate(state, 1, fluxes[2], fluxes[3], derivative, weights)
    rate_sum = rate_sum + dg_rate(state, 2, fluxes[4], fluxes[5], derivative, weights)
    return state - courant * rate_sum

def fv_next(state, fluxes, weights):
    sub_state = state
    for substep in range(SUBSTEPS):
        rate_sum = fv_rate(sub_state, 0, fluxes[0], fluxes[1], weights)
        rate_sum = rate_sum + fv_rate(sub_state, 1, fluxes[2], fluxes[3], weights)
        rate_sum = rate_sum + fv_rate(sub_state, 2, fluxes[4], fluxes[5], weights)
        sub_state = sub_state - courant / SUBSTEPS * rate_sum
    return sub_state

def z_fluxes(state):
    z_low, z_high = (state[:, :, :, 0], state[:, :, :, 3])
    below_states = jnp.concatenate([mirrored(z_low[..., 0:1]), z_high[..., :-1]], axis=-1)
    z_flux_low = rusanov(below_states, z_low, 2)
    top_flux = rusanov(z_high[..., -1:], mirrored(z_high[..., -1:]), 2)
    z_flux_high = jnp.concatenate([z_flux_low[..., 1:], top_flux], axis=-1)
    return (z_flux_low, z_flux_high, top_flux)

def wall_face_loads(z_flux_low, top_flux, weights):
    face_weights = weights[:, None] * weights[None, :]
    bottom_load = -lax.optimization_barrier(jnp.sum(face_weights[:, :, None, None] * z_flux_low[3, :, :, :, :, 0], axis=(0, 1)))
    top_load = lax.optimization_barrier(jnp.sum(face_weights[:, :, None, None] * top_flux[3, :, :, :, :, 0], axis=(0, 1)))
    return jnp.stack([bottom_load, top_load], axis=-1)

def reference(state, limit_slot, wall_owner):
    derivative, weights = gll_tables()
    x_low, x_high = (state[:, 0], state[:, 3])
    x_flux_low = rusanov(jnp.roll(x_high, 1, axis=3), x_low, 0)
    x_flux_high = jnp.roll(x_flux_low, -1, axis=3)
    y_low, y_high = (state[:, :, 0], state[:, :, 3])
    y_flux_low = rusanov(jnp.roll(y_high, 1, axis=4), y_low, 1)
    y_flux_high = jnp.roll(y_flux_low, -1, axis=4)
    z_flux_low, z_flux_high, top_flux = z_fluxes(state)
    fluxes = [x_flux_low, x_flux_high, y_flux_low, y_flux_high, z_flux_low, z_flux_high]
    dg_state = dg_next(state, fluxes, derivative, weights)
    fv_state = fv_next(state, fluxes, weights)
    state_next = jnp.where(limit_slot >= 0, fv_state, dg_state)
    face_load = wall_face_loads(z_flux_low, top_flux, weights)
    wall_loads = jax.ops.segment_sum(face_load.reshape(-1), wall_owner.reshape(-1).astype(jnp.int32), num_segments=SNODES)
    return (state_next, wall_loads)
```

```python
import functools

import jax
import jax.numpy as jnp
import numpy as np
from jax import lax
from jax.experimental import pallas as pl
from jax.experimental.pallas import tpu as pltpu
from jax.sharding import PartitionSpec as P

SUBSTEPS = 8
CAP = 16
SN_DEV = 8
LANES = 128
MESH = pl.DeviceIdType.MESH

gamma_ratio = 1.4
courant = 0.02


def gll_tables():
    nodes = np.array([-1.0, -np.sqrt(0.2), np.sqrt(0.2), 1.0])
    weights = np.array([1.0, 5.0, 5.0, 1.0]) / 6.0
    bary = np.array(
        [1.0 / np.prod([nodes[a] - nodes[b] for b in range(4) if b != a]) for a in range(4)]
    )
    derivative = np.zeros((4, 4))
    for a in range(4):
        for b in range(4):
            if a != b:
                derivative[a, b] = bary[b] / bary[a] / (nodes[a] - nodes[b])
        derivative[a, a] = -np.sum(derivative[a])
    return derivative, weights


DERIV, WEIGHTS = gll_tables()
VOLUME = DERIV.copy()
VOLUME[0, 0] += 1.0 / WEIGHTS[0]
VOLUME[3, 3] -= 1.0 / WEIGHTS[3]


def primitives(u):
    inv = 1.0 / u[0]
    p = (gamma_ratio - 1.0) * (u[4] - 0.5 * (u[1] * u[1] + u[2] * u[2] + u[3] * u[3]) * inv)
    return inv, p


def sound(inv, p):
    return jnp.sqrt(gamma_ratio * p * inv)


def flux_of(u, inv, p, d):
    v = u[1 + d] * inv
    rows = [u[1 + d]]
    for c in range(3):
        m = u[1 + c] * v
        rows.append(m + p if c == d else m)
    rows.append(v * (u[4] + p))
    return rows, v


def flux_speed(u, d):
    inv, p = primitives(u)
    rows, v = flux_of(u, inv, p, d)
    return rows, jnp.abs(v) + sound(inv, p)


def combine(ul, fl, sl, ur, fr, sr):
    half = 0.5 * jnp.maximum(sl, sr)
    return [0.5 * (fl[c] + fr[c]) - half * (ur[c] - ul[c]) for c in range(5)]


def rusanov(ul, ur, d):
    fl, sl = flux_speed(ul, d)
    fr, sr = flux_speed(ur, d)
    return combine(ul, fl, sl, ur, fr, sr)


def kernel(
    n_group,
    n_dev,
    capacity,
    state_ref,
    slot_ref,
    owner_ref,
    out_ref,
    load_ref,
    fx_ref,
    fy_ref,
    fz_ref,
    send_halo,
    recv_halo,
    part1,
    got1,
    part2,
    got2,
    hs,
    hr,
    s1,
    r1,
    s2,
    r2,
):
    gi = lax.axis_index("group")
    di = lax.axis_index("dev")

    barrier = pltpu.get_barrier_semaphore()
    for off in range(1, n_dev):
        pl.semaphore_signal(
            barrier, inc=1, device_id=(gi, lax.rem(di + off, n_dev)), device_id_type=MESH
        )
    for off in range(1, n_group):
        pl.semaphore_signal(
            barrier, inc=1, device_id=(lax.rem(gi + off, n_group), di), device_id_type=MESH
        )

    sub = lax.broadcasted_iota(jnp.int32, (8, LANES), 0)
    lane = lax.broadcasted_iota(jnp.int32, (8, LANES), 1)
    lower = sub < 4
    first = (lax.rem(sub, 4) < 2, lax.rem(sub, 2) < 1)
    shift = (2, 1)

    def tile(ref, index):
        return ref[pl.ds(pl.multiple_of(index * 8, 8), 8), :]

    def put(ref, index, value):
        ref[pl.ds(pl.multiple_of(index * 8, 8), 8), :] = value

    def node(c, i, j, kp):
        return ((c * 4 + i) * 4 + j) * 2 + kp

    def face(c, d, side, t, kp):
        return node(c, 3 * side, t, kp) if d == 0 else node(c, t, 3 * side, kp)

    roll = lambda x, n: pltpu.roll(x, n % 8, 0)

    def pack(t, carry):
        for d in range(2):
            for c in range(5):
                hi = [tile(state_ref, face(c, d, 1, t, kp)) for kp in range(2)]
                lo = [tile(state_ref, face(c, d, 0, t, kp)) for kp in range(2)]
                put(send_halo.at[2 * d + 1], c * 4 + t, jnp.where(first[d], roll(hi[0], -shift[d]), hi[1]))
                put(send_halo.at[2 * d], c * 4 + t, jnp.where(first[d], lo[0], roll(lo[1], shift[d])))
        return carry

    lax.fori_loop(0, 4, pack, 0)

    pl.semaphore_wait(barrier, n_dev - 1 + n_group - 1)

    halo_copies = []
    for d in range(2):
        for side in range(2):
            step = 1 if side == 1 else -1
            if d == 0:
                target = (lax.rem(gi + step + n_group, n_group), di)
            else:
                target = (gi, lax.rem(di + step + n_dev, n_dev))
            slot = 2 * d + side
            arrive = 2 * d + 1 - side
            copy = pltpu.make_async_remote_copy(
                src_ref=send_halo.at[slot],
                dst_ref=recv_halo.at[arrive],
                send_sem=hs.at[slot],
                recv_sem=hr.at[arrive],
                device_id=target,
                device_id_type=MESH,
            )
            copy.start()
            halo_copies.append(copy)

    wij = [[float(WEIGHTS[i] * WEIGHTS[j]) for j in range(4)] for i in range(4)]
    weight_node = lambda a: jnp.where((a == 0) | (a == 3), float(WEIGHTS[0]), float(WEIGHTS[1]))

    def z_faces(q, load):
        i, j = q // 4, q % 4
        u0 = [tile(state_ref, node(c, i, j, 0)) for c in range(5)]
        u3 = [tile(state_ref, node(c, i, j, 1)) for c in range(5)]
        below = []
        for c in range(5):
            mirror = -u0[c] if c == 3 else u0[c]
            below.append(jnp.where(lane == 0, mirror, pltpu.roll(roll(u3[c], 4), 1, 1)))
        low = rusanov(below, u0, 2)
        inv, p = primitives(u3)
        v = u3[3] * inv
        top = u3[3] * v + p + (jnp.abs(v) + sound(inv, p)) * u3[3]
        for c in range(5):
            high = pltpu.roll(roll(low[c], 4), LANES - 1, 1)
            high = jnp.where(lane == LANES - 1, top if c == 3 else 0.0, high)
            both = jnp.where(lower, low[c], high)
            put(fz_ref, node(c, i, j, 0), both)
            put(fz_ref, node(c, i, j, 1), both)
            if c == 3:
                load = load + (weight_node(i) * weight_node(j)) * both
        return load

    load = lax.fori_loop(0, 16, z_faces, jnp.zeros((8, LANES), jnp.float32))

    value = jnp.where(lower, -load, load)
    wall_lane = jnp.where(lower, 0, LANES - 1)
    value = jnp.sum(jnp.where(lane == wall_lane, value, 0.0), axis=1, keepdims=True)
    owner = jnp.zeros((8, LANES), jnp.int32)
    for s in range(2):
        for x in range(2):
            for y in range(2):
                owner = jnp.where(sub == s * 4 + x * 2 + y, owner_ref[x, y, s], owner)
    group_base = (lane // SN_DEV) * (n_dev * SN_DEV) + lax.rem(lane, SN_DEV)
    used = lane < n_group * SN_DEV
    copies1 = []
    for off in range(n_dev):
        peer = lax.rem(di + off, n_dev)
        match = (owner == group_base + peer * SN_DEV) & used
        part1[off] = jnp.where(match, value, 0.0)
        if off:
            copy = pltpu.make_async_remote_copy(
                src_ref=part1.at[off],
                dst_ref=got1.at[off],
                send_sem=s1.at[off],
                recv_sem=r1.at[off],
                device_id=(gi, peer),
                device_id_type=MESH,
            )
            copy.start()
            copies1.append(copy)

    dt = courant
    vol = [[float(VOLUME[a, b]) for b in range(4)] for a in range(4)]

    def node_flux(i, j, kp, d):
        u = [tile(state_ref, node(c, i, j, kp)) for c in range(5)]
        inv, p = primitives(u)
        return u, flux_of(u, inv, p, d)[0]

    def x_part(q, carry):
        j, kp = q // 2, q % 2
        cols = [node_flux(i, j, kp, 0) for i in range(4)]
        for c in range(5):
            for a in range(4):
                rate = sum(vol[a][b] * cols[b][1][c] for b in range(4))
                put(out_ref, node(c, a, j, kp), cols[a][0][c] - dt * rate)
        return carry

    lax.fori_loop(0, 8, x_part, 0)

    def y_part(q, carry):
        i, kp = q // 2, q % 2
        cols = [node_flux(i, j, kp, 1) for j in range(4)]
        for c in range(5):
            for a in range(4):
                rate = sum(vol[a][b] * cols[b][1][c] for b in range(4))
                index = node(c, i, a, kp)
                put(out_ref, index, tile(out_ref, index) - dt * rate)
        return carry

    lax.fori_loop(0, 8, y_part, 0)

    def halves(a, b):
        return jnp.where(lower, -dt * vol[a[0]][a[1]], -dt * vol[b[0]][b[1]])

    zc = [
        [halves((0, 0), (1, 1)), halves((0, 1), (1, 0)), halves((0, 2), (1, 3)), halves((0, 3), (1, 2))],
        [halves((2, 0), (3, 1)), halves((2, 1), (3, 0)), halves((2, 2), (3, 3)), halves((2, 3), (3, 2))],
    ]
    zf = [
        jnp.where(lower, dt / float(WEIGHTS[0]), 0.0),
        jnp.where(lower, 0.0, -dt / float(WEIGHTS[3])),
    ]

    def z_part(q, carry):
        i, j = q // 4, q % 4
        f = [node_flux(i, j, kp, 2)[1] for kp in range(2)]
        for c in range(5):
            t0, t1 = f[0][c], f[1][c]
            q0, q1 = roll(t0, 4), roll(t1, 4)
            surface = tile(fz_ref, node(c, i, j, 0))
            for kp in range(2):
                k = zc[kp]
                rate = k[0] * t0 + k[1] * q0 + k[2] * t1 + k[3] * q1 + zf[kp] * surface
                index = node(c, i, j, kp)
                put(out_ref, index, tile(out_ref, index) + rate)
        return carry

    lax.fori_loop(0, 16, z_part, 0)

    for copy in copies1:
        copy.wait()
    total = part1[0]
    for off in range(1, n_dev):
        total = total + got1[off]
    part2[...] = total
    copies2 = []
    for off in range(1, n_group):
        copy = pltpu.make_async_remote_copy(
            src_ref=part2,
            dst_ref=got2.at[off],
            send_sem=s2.at[off],
            recv_sem=r2.at[off],
            device_id=(lax.rem(gi + off, n_group), di),
            device_id_type=MESH,
        )
        copy.start()
        copies2.append(copy)

    for copy in halo_copies:
        copy.wait()

    face_scale = dt / float(WEIGHTS[0])

    def xy_faces(t, carry):
        for d in range(2):
            m, sh = first[d], shift[d]
            fref = (fx_ref, fy_ref)[d]
            own_lo = [tile(send_halo.at[2 * d], c * 4 + t) for c in range(5)]
            own_hi = [tile(send_halo.at[2 * d + 1], c * 4 + t) for c in range(5)]
            got_lo = [tile(recv_halo.at[2 * d], c * 4 + t) for c in range(5)]
            got_hi = [tile(recv_halo.at[2 * d + 1], c * 4 + t) for c in range(5)]
            left, right = [], []
            for c in range(5):
                hi = [tile(state_ref, face(c, d, 1, t, kp)) for kp in range(2)]
                lo = [tile(state_ref, face(c, d, 0, t, kp)) for kp in range(2)]
                left.append(jnp.where(m, hi[0], roll(hi[1], sh)))
                right.append(jnp.where(m, roll(lo[0], -sh), lo[1]))
            flo = rusanov(got_lo, own_lo, d)
            fin = rusanov(left, right, d)
            fhi = rusanov(own_hi, got_hi, d)
            for c in range(5):
                down, up = roll(fin[c], -sh), roll(fin[c], sh)
                values = [
                    [jnp.where(m, flo[c], up), jnp.where(m, roll(flo[c], -sh), fin[c])],
                    [jnp.where(m, fin[c], roll(fhi[c], sh)), jnp.where(m, down, fhi[c])],
                ]
                for side in range(2):
                    for kp in range(2):
                        val = values[side][kp]
                        if d == 0:
                            put(fref, ((c * 2 + side) * 4 + t) * 2 + kp, val)
                        else:
                            put(fref, ((c * 4 + t) * 2 + side) * 2 + kp, val)
                        index = face(c, d, side, t, kp)
                        scaled = face_scale * val
                        old = tile(out_ref, index)
                        put(out_ref, index, old - scaled if side else old + scaled)
        return carry

    lax.fori_loop(0, 4, xy_faces, 0)

    def split(x):
        hi = x.astype(jnp.bfloat16)
        return hi, (x - hi.astype(jnp.float32)).astype(jnp.bfloat16)

    kmod = lax.rem(sub, 4)
    k_first, k_last = kmod == 0, kmod == 3
    edge, inner = 1.0 / float(WEIGHTS[0]), 1.0 / float(WEIGHTS[1])
    sub_dt = courant / SUBSTEPS
    wk = jnp.where(k_first | k_last, sub_dt * edge, sub_dt * inner)
    wj = [
        jnp.where(lower, sub_dt * edge, sub_dt * inner),
        jnp.where(lower, sub_dt * inner, sub_dt * edge),
    ]
    wi = [sub_dt * edge, sub_dt * inner, sub_dt * inner, sub_dt * edge]

    for block in range(-(-capacity // LANES)):
        base = block * LANES
        rank = lax.broadcasted_iota(jnp.int32, (LANES, LANES), 0) + base
        slots = [slot_ref[e // 2, pl.ds(e % 2, 1), :] for e in range(4)]
        onehot = jnp.concatenate(
            [jnp.where(rank == s, 1.0, 0.0).astype(jnp.bfloat16) for s in slots], axis=1
        )

        def gather(ref, rows):
            x = jnp.concatenate(
                [ref[pl.ds(e, rows, stride=4), :] for e in range(4)], axis=1
            )
            dims = (((1,), (1,)), ((), ()))
            hi, mid = split(x)
            return lax.dot_general(
                hi, onehot, dims, preferred_element_type=jnp.float32
            ) + lax.dot_general(mid, onehot, dims, preferred_element_type=jnp.float32)

        packed = gather(state_ref, 320)
        occupied = packed[0:1, :] > 0.25
        px = gather(fx_ref, 160)
        py = gather(fy_ref, 160)
        pz = gather(fz_ref, 320)
        cut = lambda a, t: a[8 * t : 8 * t + 8]
        blank = (1.0, 0.0, 0.0, 0.0, 2.5)
        start = tuple(
            jnp.where(occupied, cut(packed, c * 8 + t), blank[c])
            for c in range(5)
            for t in range(8)
        )

        def substep(_, flat):
            u = [[flat[c * 8 + t] for c in range(5)] for t in range(8)]
            prim = [primitives(u[t]) for t in range(8)]
            cs = [sound(*prim[t]) for t in range(8)]
            new = [list(u[t]) for t in range(8)]

            def fluxes(d):
                out = []
                for t in range(8):
                    rows, v = flux_of(u[t], prim[t][0], prim[t][1], d)
                    out.append((rows, jnp.abs(v) + cs[t]))
                return out

            f = fluxes(0)
            for jp in range(2):
                g = [[cut(px, (c * 2 + 0) * 2 + jp) for c in range(5)]]
                for a in range(3):
                    l, r = a * 2 + jp, (a + 1) * 2 + jp
                    g.append(combine(u[l], f[l][0], f[l][1], u[r], f[r][0], f[r][1]))
                g.append([cut(px, (c * 2 + 1) * 2 + jp) for c in range(5)])
                for a in range(4):
                    t = a * 2 + jp
                    for c in range(5):
                        new[t][c] = new[t][c] - wi[a] * (g[a + 1][c] - g[a][c])

            f = fluxes(1)
            for i in range(4):
                t0, t1 = 2 * i, 2 * i + 1
                rolled = []
                for t in (t0, t1):
                    rolled.append(
                        (
                            [roll(x, 4) for x in u[t]],
                            [roll(x, 4) for x in f[t][0]],
                            roll(f[t][1], 4),
                        )
                    )
                ra, rb = rolled
                mix = lambda a, b: [jnp.where(lower, x, y) for x, y in zip(a, b)]
                ga = combine(
                    u[t0], f[t0][0], f[t0][1],
                    mix(ra[0], rb[0]), mix(ra[1], rb[1]), jnp.where(lower, ra[2], rb[2]),
                )
                gb = combine(u[t1], f[t1][0], f[t1][1], rb[0], rb[1], rb[2])
                for c in range(5):
                    bound = cut(py, c * 4 + i)
                    high1 = jnp.where(lower, gb[c], bound)
                    back0, back1 = roll(ga[c], 4), roll(high1, 4)
                    low0 = jnp.where(lower, bound, back0)
                    low1 = jnp.where(lower, back0, back1)
                    new[t0][c] = new[t0][c] - wj[0] * (ga[c] - low0)
                    new[t1][c] = new[t1][c] - wj[1] * (high1 - low1)

            f = fluxes(2)
            for t in range(8):
                g = combine(
                    u[t], f[t][0], f[t][1],
                    [roll(x, -1) for x in u[t]], [roll(x, -1) for x in f[t][0]], roll(f[t][1], -1),
                )
                for c in range(5):
                    bound = cut(pz, c * 8 + t)
                    high = jnp.where(k_last, bound, g[c])
                    low = jnp.where(k_first, bound, roll(high, 1))
                    new[t][c] = new[t][c] - wk * (high - low)
            return tuple(new[t][c] for c in range(5) for t in range(8))

        final = lax.fori_loop(0, SUBSTEPS, substep, start)
        result = jnp.concatenate([jnp.where(occupied, x, 0.0) for x in final], axis=0)
        hi, mid = split(result)
        dims = (((1,), (0,)), ((), ()))
        spread = lax.dot_general(
            hi, onehot, dims, preferred_element_type=jnp.float32
        ) + lax.dot_general(mid, onehot, dims, preferred_element_type=jnp.float32)
        for e in range(4):
            rows = pl.ds(e, 320, stride=4)
            here = (slots[e] >= base) & (slots[e] < base + LANES)
            out_ref[rows, :] = jnp.where(
                here, spread[:, e * LANES : (e + 1) * LANES], out_ref[rows, :]
            )

    for copy in copies2:
        copy.wait()
    total = part2[...]
    for off in range(1, n_group):
        total = total + got2[off]
    row = jnp.sum(total, axis=0, keepdims=True)
    mine = jnp.zeros((1, SN_DEV), jnp.float32)
    for g in range(n_group):
        mine = jnp.where(gi == g, row[:, g * SN_DEV : (g + 1) * SN_DEV], mine)
    load_ref[...] = mine


def on_device(n_group, n_dev, state, limit_slot, wall_owner):
    rows = state.size // LANES
    f32 = jnp.float32
    vmem = pl.BlockSpec(memory_space=pltpu.VMEM)
    out, loads = pl.pallas_call(
        functools.partial(kernel, n_group, n_dev, n_dev * CAP),
        out_shape=(
            jax.ShapeDtypeStruct((rows, LANES), f32),
            jax.ShapeDtypeStruct((1, SN_DEV), f32),
        ),
        in_specs=[vmem, vmem, pl.BlockSpec(memory_space=pltpu.SMEM)],
        out_specs=(vmem, vmem),
        scratch_shapes=[
            pltpu.VMEM((640, LANES), f32),
            pltpu.VMEM((640, LANES), f32),
            pltpu.VMEM((rows, LANES), f32),
            pltpu.VMEM((4, 160, LANES), f32),
            pltpu.VMEM((4, 160, LANES), f32),
            pltpu.VMEM((n_dev, 8, LANES), f32),
            pltpu.VMEM((n_dev, 8, LANES), f32),
            pltpu.VMEM((8, LANES), f32),
            pltpu.VMEM((n_group, 8, LANES), f32),
            pltpu.SemaphoreType.DMA((4,)),
            pltpu.SemaphoreType.DMA((4,)),
            pltpu.SemaphoreType.DMA((n_dev,)),
            pltpu.SemaphoreType.DMA((n_dev,)),
            pltpu.SemaphoreType.DMA((n_group,)),
            pltpu.SemaphoreType.DMA((n_group,)),
        ],
        compiler_params=pltpu.CompilerParams(
            collective_id=0, has_side_effects=True, vmem_limit_bytes=32 * 1024 * 1024
        ),
    )(state.reshape(rows, LANES), limit_slot, wall_owner)
    return out.reshape(state.shape), loads.reshape(SN_DEV)


def solution(mesh):
    in_specs = (
        P(None, None, None, None, "group", "dev", None),
        P("group", "dev", None),
        P("group", "dev", None),
    )
    out_specs = (P(None, None, None, None, "group", "dev", None), P(("group", "dev")))
    return jax.shard_map(
        functools.partial(on_device, mesh.shape["group"], mesh.shape["dev"]),
        mesh=mesh, in_specs=in_specs, out_specs=out_specs, check_vma=False,
    )
```

```python
import functools

import jax
import jax.numpy as jnp
import numpy as np
from jax import lax
from jax.experimental import pallas as pl
from jax.experimental.pallas import tpu as pltpu
from jax.sharding import PartitionSpec as P

SUBSTEPS = 8
CAP = 16
SN_DEV = 8
LANES = 128
MESH = pl.DeviceIdType.MESH

gamma_ratio = 1.4
courant = 0.02


def gll_tables():
    nodes = np.array([-1.0, -np.sqrt(0.2), np.sqrt(0.2), 1.0])
    weights = np.array([1.0, 5.0, 5.0, 1.0]) / 6.0
    bary = np.array(
        [1.0 / np.prod([nodes[a] - nodes[b] for b in range(4) if b != a]) for a in range(4)]
    )
    derivative = np.zeros((4, 4))
    for a in range(4):
        for b in range(4):
            if a != b:
                derivative[a, b] = bary[b] / bary[a] / (nodes[a] - nodes[b])
        derivative[a, a] = -np.sum(derivative[a])
    return derivative, weights


DERIV, WEIGHTS = gll_tables()
VOLUME = DERIV.copy()
VOLUME[0, 0] += 1.0 / WEIGHTS[0]
VOLUME[3, 3] -= 1.0 / WEIGHTS[3]


def primitives(u):
    inv = 1.0 / u[0]
    p = (gamma_ratio - 1.0) * (u[4] - 0.5 * (u[1] * u[1] + u[2] * u[2] + u[3] * u[3]) * inv)
    return inv, p


def sound(inv, p):
    return jnp.sqrt(gamma_ratio * p * inv)


def flux_of(u, inv, p, d):
    v = u[1 + d] * inv
    rows = [u[1 + d]]
    for c in range(3):
        m = u[1 + c] * v
        rows.append(m + p if c == d else m)
    rows.append(v * (u[4] + p))
    return rows, v


def flux_speed(u, d):
    inv, p = primitives(u)
    rows, v = flux_of(u, inv, p, d)
    return rows, jnp.abs(v) + sound(inv, p)


def combine(ul, fl, sl, ur, fr, sr):
    half = 0.5 * jnp.maximum(sl, sr)
    return [0.5 * (fl[c] + fr[c]) - half * (ur[c] - ul[c]) for c in range(5)]


def combine_twice(ul, fl, sl, ur, fr, sr):
    fastest = jnp.maximum(sl, sr)
    return [(fl[c] + fr[c]) - fastest * (ur[c] - ul[c]) for c in range(5)]


def rusanov(ul, ur, d):
    fl, sl = flux_speed(ul, d)
    fr, sr = flux_speed(ur, d)
    return combine(ul, fl, sl, ur, fr, sr)


def kernel(
    n_group,
    n_dev,
    capacity,
    state_ref,
    slot_ref,
    owner_ref,
    out_ref,
    load_ref,
    fx_ref,
    fy_ref,
    fz_ref,
    send_halo,
    recv_halo,
    part1,
    got1,
    part2,
    got2,
    hs,
    hr,
    s1,
    r1,
    s2,
    r2,
):
    gi = lax.axis_index("group")
    di = lax.axis_index("dev")

    barrier = pltpu.get_barrier_semaphore()
    for off in range(1, n_dev):
        pl.semaphore_signal(
            barrier, inc=1, device_id=(gi, lax.rem(di + off, n_dev)), device_id_type=MESH
        )
    for off in range(1, n_group):
        pl.semaphore_signal(
            barrier, inc=1, device_id=(lax.rem(gi + off, n_group), di), device_id_type=MESH
        )

    sub = lax.broadcasted_iota(jnp.int32, (8, LANES), 0)
    lane = lax.broadcasted_iota(jnp.int32, (8, LANES), 1)
    lower = sub < 4
    first = (lax.rem(sub, 4) < 2, lax.rem(sub, 2) < 1)
    shift = (2, 1)

    def tile(ref, index):
        return ref[pl.ds(pl.multiple_of(index * 8, 8), 8), :]

    def put(ref, index, value):
        ref[pl.ds(pl.multiple_of(index * 8, 8), 8), :] = value

    def node(c, i, j, kp):
        return ((c * 4 + i) * 4 + j) * 2 + kp

    def face(c, d, side, t, kp):
        return node(c, 3 * side, t, kp) if d == 0 else node(c, t, 3 * side, kp)

    roll = lambda x, n: pltpu.roll(x, n % 8, 0)

    def pack(t, carry):
        for d in range(2):
            for c in range(5):
                hi = [tile(state_ref, face(c, d, 1, t, kp)) for kp in range(2)]
                lo = [tile(state_ref, face(c, d, 0, t, kp)) for kp in range(2)]
                put(send_halo.at[2 * d + 1], c * 4 + t, jnp.where(first[d], roll(hi[0], -shift[d]), hi[1]))
                put(send_halo.at[2 * d], c * 4 + t, jnp.where(first[d], lo[0], roll(lo[1], shift[d])))
        return carry

    lax.fori_loop(0, 4, pack, 0)

    wij = [[float(WEIGHTS[i] * WEIGHTS[j]) for j in range(4)] for i in range(4)]
    weight_node = lambda a: jnp.where((a == 0) | (a == 3), float(WEIGHTS[0]), float(WEIGHTS[1]))

    def z_faces(q, load):
        i, j = q // 4, q % 4
        u0 = [tile(state_ref, node(c, i, j, 0)) for c in range(5)]
        u3 = [tile(state_ref, node(c, i, j, 1)) for c in range(5)]
        below = []
        for c in range(5):
            mirror = -u0[c] if c == 3 else u0[c]
            below.append(jnp.where(lane == 0, mirror, pltpu.roll(roll(u3[c], 4), 1, 1)))
        low = rusanov(below, u0, 2)
        inv, p = primitives(u3)
        v = u3[3] * inv
        top = u3[3] * v + p + (jnp.abs(v) + sound(inv, p)) * u3[3]
        for c in range(5):
            high = pltpu.roll(roll(low[c], 4), LANES - 1, 1)
            high = jnp.where(lane == LANES - 1, top if c == 3 else 0.0, high)
            both = jnp.where(lower, low[c], high)
            put(fz_ref, node(c, i, j, 0), both)
            put(fz_ref, node(c, i, j, 1), both)
            if c == 3:
                load = load + (weight_node(i) * weight_node(j)) * both
        return load

    load = lax.fori_loop(0, 16, z_faces, jnp.zeros((8, LANES), jnp.float32), unroll=4)

    value = jnp.where(lower, -load, load)
    wall_lane = jnp.where(lower, 0, LANES - 1)
    value = jnp.sum(jnp.where(lane == wall_lane, value, 0.0), axis=1, keepdims=True)
    owner = jnp.zeros((8, LANES), jnp.int32)
    for s in range(2):
        for x in range(2):
            for y in range(2):
                owner = jnp.where(sub == s * 4 + x * 2 + y, owner_ref[x, y, s], owner)
    group_base = (lane // SN_DEV) * (n_dev * SN_DEV) + lax.rem(lane, SN_DEV)
    used = lane < n_group * SN_DEV
    for off in range(n_dev):
        peer = lax.rem(di + off, n_dev)
        match = (owner == group_base + peer * SN_DEV) & used
        part1[off] = jnp.where(match, value, 0.0)

    pl.semaphore_wait(barrier, n_dev - 1 + n_group - 1)

    halo_copies = []
    for d in range(2):
        for side in range(2):
            step = 1 if side == 1 else -1
            if d == 0:
                target = (lax.rem(gi + step + n_group, n_group), di)
            else:
                target = (gi, lax.rem(di + step + n_dev, n_dev))
            slot = 2 * d + side
            arrive = 2 * d + 1 - side
            copy = pltpu.make_async_remote_copy(
                src_ref=send_halo.at[slot],
                dst_ref=recv_halo.at[arrive],
                send_sem=hs.at[slot],
                recv_sem=hr.at[arrive],
                device_id=target,
                device_id_type=MESH,
            )
            copy.start()
            halo_copies.append(copy)

    copies1 = []
    for off in range(1, n_dev):
        copy = pltpu.make_async_remote_copy(
            src_ref=part1.at[off],
            dst_ref=got1.at[off],
            send_sem=s1.at[off],
            recv_sem=r1.at[off],
            device_id=(gi, lax.rem(di + off, n_dev)),
            device_id_type=MESH,
        )
        copy.start()
        copies1.append(copy)

    dt = courant
    vol = [[float(VOLUME[a, b]) for b in range(4)] for a in range(4)]

    def node_flux(i, j, kp, d):
        u = [tile(state_ref, node(c, i, j, kp)) for c in range(5)]
        inv, p = primitives(u)
        return u, flux_of(u, inv, p, d)[0]

    def x_part(q, carry):
        j, kp = q // 2, q % 2
        cols = [node_flux(i, j, kp, 0) for i in range(4)]
        for c in range(5):
            for a in range(4):
                rate = sum(vol[a][b] * cols[b][1][c] for b in range(4))
                put(out_ref, node(c, a, j, kp), cols[a][0][c] - dt * rate)
        return carry

    lax.fori_loop(0, 8, x_part, 0, unroll=2)

    def y_part(q, carry):
        i, kp = q // 2, q % 2
        cols = [node_flux(i, j, kp, 1) for j in range(4)]
        for c in range(5):
            for a in range(4):
                rate = sum(vol[a][b] * cols[b][1][c] for b in range(4))
                index = node(c, i, a, kp)
                put(out_ref, index, tile(out_ref, index) - dt * rate)
        return carry

    lax.fori_loop(0, 8, y_part, 0, unroll=2)

    def halves(a, b):
        return jnp.where(lower, -dt * vol[a[0]][a[1]], -dt * vol[b[0]][b[1]])

    zc = [
        [halves((0, 0), (1, 1)), halves((0, 1), (1, 0)), halves((0, 2), (1, 3)), halves((0, 3), (1, 2))],
        [halves((2, 0), (3, 1)), halves((2, 1), (3, 0)), halves((2, 2), (3, 3)), halves((2, 3), (3, 2))],
    ]
    zf = [
        jnp.where(lower, dt / float(WEIGHTS[0]), 0.0),
        jnp.where(lower, 0.0, -dt / float(WEIGHTS[3])),
    ]

    def z_part(q, carry):
        i, j = q // 4, q % 4
        f = [node_flux(i, j, kp, 2)[1] for kp in range(2)]
        for c in range(5):
            t0, t1 = f[0][c], f[1][c]
            q0, q1 = roll(t0, 4), roll(t1, 4)
            surface = tile(fz_ref, node(c, i, j, 0))
            for kp in range(2):
                k = zc[kp]
                rate = k[0] * t0 + k[1] * q0 + k[2] * t1 + k[3] * q1 + zf[kp] * surface
                index = node(c, i, j, kp)
                put(out_ref, index, tile(out_ref, index) + rate)
        return carry

    lax.fori_loop(0, 16, z_part, 0, unroll=4)

    for copy in copies1:
        copy.wait()
    total = part1[0]
    for off in range(1, n_dev):
        total = total + got1[off]
    part2[...] = total
    copies2 = []
    for off in range(1, n_group):
        copy = pltpu.make_async_remote_copy(
            src_ref=part2,
            dst_ref=got2.at[off],
            send_sem=s2.at[off],
            recv_sem=r2.at[off],
            device_id=(lax.rem(gi + off, n_group), di),
            device_id_type=MESH,
        )
        copy.start()
        copies2.append(copy)

    for copy in halo_copies:
        copy.wait()

    face_scale = dt / float(WEIGHTS[0])

    def xy_faces(t, carry):
        for d in range(2):
            m, sh = first[d], shift[d]
            fref = (fx_ref, fy_ref)[d]
            own_lo = [tile(send_halo.at[2 * d], c * 4 + t) for c in range(5)]
            own_hi = [tile(send_halo.at[2 * d + 1], c * 4 + t) for c in range(5)]
            got_lo = [tile(recv_halo.at[2 * d], c * 4 + t) for c in range(5)]
            got_hi = [tile(recv_halo.at[2 * d + 1], c * 4 + t) for c in range(5)]
            left, right = [], []
            for c in range(5):
                hi = [tile(state_ref, face(c, d, 1, t, kp)) for kp in range(2)]
                lo = [tile(state_ref, face(c, d, 0, t, kp)) for kp in range(2)]
                left.append(jnp.where(m, hi[0], roll(hi[1], sh)))
                right.append(jnp.where(m, roll(lo[0], -sh), lo[1]))
            flo = rusanov(got_lo, own_lo, d)
            fin = rusanov(left, right, d)
            fhi = rusanov(own_hi, got_hi, d)
            for c in range(5):
                down, up = roll(fin[c], -sh), roll(fin[c], sh)
                values = [
                    [jnp.where(m, flo[c], up), jnp.where(m, roll(flo[c], -sh), fin[c])],
                    [jnp.where(m, fin[c], roll(fhi[c], sh)), jnp.where(m, down, fhi[c])],
                ]
                for side in range(2):
                    for kp in range(2):
                        val = values[side][kp]
                        if d == 0:
                            put(fref, ((c * 2 + side) * 4 + t) * 2 + kp, val)
                        else:
                            put(fref, ((c * 4 + t) * 2 + side) * 2 + kp, val)
                        index = face(c, d, side, t, kp)
                        scaled = face_scale * val
                        old = tile(out_ref, index)
                        put(out_ref, index, old - scaled if side else old + scaled)
        return carry

    lax.fori_loop(0, 4, xy_faces, 0)

    def split(x):
        hi = x.astype(jnp.bfloat16)
        return hi, (x - hi.astype(jnp.float32)).astype(jnp.bfloat16)

    kmod = lax.rem(sub, 4)
    k_first, k_last = kmod == 0, kmod == 3
    edge, inner = 1.0 / float(WEIGHTS[0]), 1.0 / float(WEIGHTS[1])
    sub_dt = 0.5 * courant / SUBSTEPS
    wk = jnp.where(k_first | k_last, sub_dt * edge, sub_dt * inner)
    wj = [
        jnp.where(lower, sub_dt * edge, sub_dt * inner),
        jnp.where(lower, sub_dt * inner, sub_dt * edge),
    ]
    wi = [sub_dt * edge, sub_dt * inner, sub_dt * inner, sub_dt * edge]

    for block in range(-(-capacity // LANES)):
        base = block * LANES
        rank = lax.broadcasted_iota(jnp.int32, (LANES, LANES), 0) + base
        slots = [slot_ref[e // 2, pl.ds(e % 2, 1), :] for e in range(4)]
        onehot = jnp.concatenate(
            [jnp.where(rank == s, 1.0, 0.0).astype(jnp.bfloat16) for s in slots], axis=1
        )

        def gather(ref, rows):
            x = jnp.concatenate(
                [ref[pl.ds(e, rows, stride=4), :] for e in range(4)], axis=1
            )
            dims = (((1,), (1,)), ((), ()))
            hi, mid = split(x)
            return lax.dot_general(
                hi, onehot, dims, preferred_element_type=jnp.float32
            ) + lax.dot_general(mid, onehot, dims, preferred_element_type=jnp.float32)

        packed = gather(state_ref, 320)
        occupied = packed[0:1, :] > 0.25
        px = gather(fx_ref, 160)
        py = gather(fy_ref, 160)
        pz = gather(fz_ref, 320)
        cut = lambda a, t: a[8 * t : 8 * t + 8]
        blank = (1.0, 0.0, 0.0, 0.0, 2.5)
        start = tuple(
            jnp.where(occupied, cut(packed, c * 8 + t), blank[c])
            for c in range(5)
            for t in range(8)
        )

        px, py, pz = px + px, py + py, pz + pz

        def substep(_, flat):
            u = [[flat[c * 8 + t] for c in range(5)] for t in range(8)]
            prim = [primitives(u[t]) for t in range(8)]
            cs = [sound(*prim[t]) for t in range(8)]
            new = [list(u[t]) for t in range(8)]

            def fluxes(d):
                out = []
                for t in range(8):
                    rows, v = flux_of(u[t], prim[t][0], prim[t][1], d)
                    out.append((rows, jnp.abs(v) + cs[t]))
                return out

            f = fluxes(0)
            for jp in range(2):
                g = [[cut(px, (c * 2 + 0) * 2 + jp) for c in range(5)]]
                for a in range(3):
                    l, r = a * 2 + jp, (a + 1) * 2 + jp
                    g.append(combine_twice(u[l], f[l][0], f[l][1], u[r], f[r][0], f[r][1]))
                g.append([cut(px, (c * 2 + 1) * 2 + jp) for c in range(5)])
                for a in range(4):
                    t = a * 2 + jp
                    for c in range(5):
                        new[t][c] = new[t][c] - wi[a] * (g[a + 1][c] - g[a][c])

            f = fluxes(1)
            for i in range(4):
                t0, t1 = 2 * i, 2 * i + 1
                rolled = []
                for t in (t0, t1):
                    rolled.append(
                        (
                            [roll(x, 4) for x in u[t]],
                            [roll(x, 4) for x in f[t][0]],
                            roll(f[t][1], 4),
                        )
                    )
                ra, rb = rolled
                mix = lambda a, b: [jnp.where(lower, x, y) for x, y in zip(a, b)]
                ga = combine_twice(
                    u[t0], f[t0][0], f[t0][1],
                    mix(ra[0], rb[0]), mix(ra[1], rb[1]), jnp.where(lower, ra[2], rb[2]),
                )
                gb = combine_twice(u[t1], f[t1][0], f[t1][1], rb[0], rb[1], rb[2])
                for c in range(5):
                    bound = cut(py, c * 4 + i)
                    high1 = jnp.where(lower, gb[c], bound)
                    back0, back1 = roll(ga[c], 4), roll(high1, 4)
                    low0 = jnp.where(lower, bound, back0)
                    low1 = jnp.where(lower, back0, back1)
                    new[t0][c] = new[t0][c] - wj[0] * (ga[c] - low0)
                    new[t1][c] = new[t1][c] - wj[1] * (high1 - low1)

            f = fluxes(2)
            for t in range(8):
                g = combine_twice(
                    u[t], f[t][0], f[t][1],
                    [roll(x, -1) for x in u[t]], [roll(x, -1) for x in f[t][0]], roll(f[t][1], -1),
                )
                for c in range(5):
                    bound = cut(pz, c * 8 + t)
                    high = jnp.where(k_last, bound, g[c])
                    low = jnp.where(k_first, bound, roll(high, 1))
                    new[t][c] = new[t][c] - wk * (high - low)
            return tuple(new[t][c] for c in range(5) for t in range(8))

        final = lax.fori_loop(0, SUBSTEPS, substep, start)
        result = jnp.concatenate([jnp.where(occupied, x, 0.0) for x in final], axis=0)
        hi, mid = split(result)
        dims = (((1,), (0,)), ((), ()))
        spread = lax.dot_general(
            hi, onehot, dims, preferred_element_type=jnp.float32
        ) + lax.dot_general(mid, onehot, dims, preferred_element_type=jnp.float32)
        for e in range(4):
            rows = pl.ds(e, 320, stride=4)
            here = (slots[e] >= base) & (slots[e] < base + LANES)
            out_ref[rows, :] = jnp.where(
                here, spread[:, e * LANES : (e + 1) * LANES], out_ref[rows, :]
            )

    for copy in copies2:
        copy.wait()
    total = part2[...]
    for off in range(1, n_group):
        total = total + got2[off]
    row = jnp.sum(total, axis=0, keepdims=True)
    mine = jnp.zeros((1, SN_DEV), jnp.float32)
    for g in range(n_group):
        mine = jnp.where(gi == g, row[:, g * SN_DEV : (g + 1) * SN_DEV], mine)
    load_ref[...] = mine


def on_device(n_group, n_dev, state, limit_slot, wall_owner):
    rows = state.size // LANES
    f32 = jnp.float32
    vmem = pl.BlockSpec(memory_space=pltpu.VMEM)
    out, loads = pl.pallas_call(
        functools.partial(kernel, n_group, n_dev, n_dev * CAP),
        out_shape=(
            jax.ShapeDtypeStruct((rows, LANES), f32),
            jax.ShapeDtypeStruct((1, SN_DEV), f32),
        ),
        in_specs=[vmem, vmem, pl.BlockSpec(memory_space=pltpu.SMEM)],
        out_specs=(vmem, vmem),
        scratch_shapes=[
            pltpu.VMEM((640, LANES), f32),
            pltpu.VMEM((640, LANES), f32),
            pltpu.VMEM((rows, LANES), f32),
            pltpu.VMEM((4, 160, LANES), f32),
            pltpu.VMEM((4, 160, LANES), f32),
            pltpu.VMEM((n_dev, 8, LANES), f32),
            pltpu.VMEM((n_dev, 8, LANES), f32),
            pltpu.VMEM((8, LANES), f32),
            pltpu.VMEM((n_group, 8, LANES), f32),
            pltpu.SemaphoreType.DMA((4,)),
            pltpu.SemaphoreType.DMA((4,)),
            pltpu.SemaphoreType.DMA((n_dev,)),
            pltpu.SemaphoreType.DMA((n_dev,)),
            pltpu.SemaphoreType.DMA((n_group,)),
            pltpu.SemaphoreType.DMA((n_group,)),
        ],
        compiler_params=pltpu.CompilerParams(
            collective_id=0, has_side_effects=True, vmem_limit_bytes=32 * 1024 * 1024
        ),
    )(state.reshape(rows, LANES), limit_slot, wall_owner)
    return out.reshape(state.shape), loads.reshape(SN_DEV)


def solution(mesh):
    in_specs = (
        P(None, None, None, None, "group", "dev", None),
        P("group", "dev", None),
        P("group", "dev", None),
    )
    out_specs = (P(None, None, None, None, "group", "dev", None), P(("group", "dev")))
    return jax.shard_map(
        functools.partial(on_device, mesh.shape["group"], mesh.shape["dev"]),
        mesh=mesh, in_specs=in_specs, out_specs=out_specs, check_vma=False,
    )
```
